256 devices in a mesh: dp: 32 (over y, z_hi, core), tensor: 8 (over x, z_lo).
Axes of the slice: x: 4, y: 4, z: 8 (z_hi: 4, z_lo: 2; z = z_hi * 2 + z_lo), core: 2. Of those that a mesh axis runs over, the one named last changes fastest.
Arguments:
- layer_input: bfloat16 [16384, 8192], P('dp', 'tensor'), may hold values from -6 to 6
- hidden_act: bfloat16 [16384, 28672], P('dp', 'tensor'), may hold values from -6 to 6
- grad_gate: bfloat16 [16384, 28672], P('dp', 'tensor'), may hold values from -6 to 6
- grad_up: bfloat16 [16384, 28672], P('dp', 'tensor'), may hold values from -6 to 6
- grad_output: bfloat16 [16384, 8192], P('dp', 'tensor'), may hold values from -6 to 6
- proj_gate_in: bfloat16 [8192, 64], P('tensor'), may hold values from -0.0625 to 0.0625
- proj_up_in: bfloat16 [8192, 64], P('tensor'), may hold values from -0.0625 to 0.0625
- proj_down_in: bfloat16 [28672, 64], P('tensor'), may hold values from -0.03125 to 0.03125
- proj_gate_out: bfloat16 [28672, 64], P('tensor'), may hold values from -0.03125 to 0.03125
- proj_up_out: bfloat16 [28672, 64], P('tensor'), may hold values from -0.03125 to 0.03125
- proj_down_out: bfloat16 [8192, 64], P('tensor'), may hold values from -0.0625 to 0.0625
- example_ids: int32 [32, 512], P('dp'), may hold values from 0 to 15, never falling along the last dimension, each value on 1 to 64 neighbouring positions
- query_sketches: bfloat16 [4096, 12288], P('dp', 'tensor'), may hold values from -0.019897461 to 0.019897461
Outputs:
- sketches: bfloat16 [512, 12288], P('dp', 'tensor')
- scores: float32 [512, 4096], P('dp', 'tensor')
The draws below stay inside these ranges and needn't reach their ends.
Inputs may be any that keep to these rules, and one draw needn't show every extreme that they name: `example_ids`: in each row the ids never fall and every id from 0 to 15 occurs.
All inputs are finite; a program needn't handle non-finite values.
Results may differ from the reference program's by a relative error of at most 0.0058.
Values may be sent and summed in bfloat16 or wider, within the bound.
No kernel may reach another device: no remote copies, remote signals or barrier semaphores. Data moves between devices by JAX's collectives and lax.ppermute only.
A program may use at most 128 MiB of HBM per device.

```python
import math
import jax
import jax.numpy as jnp
import numpy as np
from jax import lax

D = 8192
FF = 28672
RANK = 64
TOK = 512
EX_DEV = 16
GROUPS = 32
TOKENS = 16384
EXAMPLES = 512
QUERIES = 4096
SKETCH = 12288


def block_levels(stream_key, extent, cuts, smallest, top_value):
    def one(axis_at, parts):
        steps = jax.random.uniform(jax.random.fold_in(jax.random.fold_in(stream_key, 6), axis_at), (parts,), jnp.float32, smallest / len(cuts), top_value / len(cuts))
        return jnp.repeat(jnp.exp(steps), extent[axis_at] // parts).reshape((-1,) + (1,) * (len(extent) - axis_at - 1))

    factor_of = one(*cuts[0])
    for cut in cuts[1:]:
        factor_of = factor_of * one(*cut)
    return factor_of


def split_up(count, total, limit, skew):
    weights = [(1 << 20) // math.isqrt(standing ** skew) + 1 for standing in range(2, count + 1)]
    surplus, given = total - limit - (count - 1), [1] * (count - 1)
    while surplus > 0:
        free = [i for i in range(count - 1) if given[i] < limit]
        whole, budget = sum([weights[i] for i in free]), surplus
        for i in free:
            extra = min(limit - given[i], max(1, budget * weights[i] // whole), surplus)
            given[i] = given[i] + extra
            surplus = surplus - extra
    return np.array([limit] + given)


def ragged_sizes(own_key, amount, total, reach, lean):
    if amount == 2:
        one = jax.random.randint(own_key, (), max(1, total - reach), min(reach, total - 1) + 1)
        return jnp.stack([one, total - one])
    tallies = jnp.asarray(split_up(amount, total, reach, lean), jnp.int32)
    pairs = (amount - 1) // 2
    source_of, receiver = tallies[1:1 + 2 * pairs:2], tallies[2:2 + 2 * pairs:2]
    room = jnp.minimum(source_of - 1, reach - receiver)
    moved = jax.random.randint(jax.random.fold_in(own_key, 1), (pairs,), 0, 1 << 20) % (room + 1)
    tallies = tallies.at[1:1 + 2 * pairs:2].set(source_of - moved).at[2:2 + 2 * pairs:2].set(receiver + moved)
    return tallies[jax.random.permutation(jax.random.fold_in(own_key, 2), amount)]


def noise(key, shape, deviation, limit, cuts=(), held_as=jnp.bfloat16):
    gain = block_levels(key, shape, cuts, -0.22, 0.18) if cuts else 1.0
    array = jax.random.normal(key, shape, jnp.float32) * deviation * gain
    return jnp.minimum(jnp.maximum(array, -limit), limit).astype(held_as)


def setup_inputs(seed: int = 0) -> dict:
    arg_keys = jax.random.split(jax.random.key(seed), 14)
    return {
        "layer_input": noise(arg_keys[0], (TOKENS, D), 1.0, 6.0, ((0, 32), (1, 8))),
        "hidden_act": noise(arg_keys[1], (TOKENS, FF), 1.0, 6.0, ((0, 32), (1, 8))),
        "grad_gate": noise(arg_keys[2], (TOKENS, FF), 1.0, 6.0, ((0, 32), (1, 8))),
        "grad_up": noise(arg_keys[3], (TOKENS, FF), 1.0, 6.0, ((0, 32), (1, 8))),
        "grad_output": noise(arg_keys[4], (TOKENS, D), 1.0, 6.0, ((0, 32), (1, 8))),
        "proj_gate_in": noise(arg_keys[5], (D, RANK), D ** -0.5, 0.0625, ((0, 8),)),
        "proj_up_in": noise(arg_keys[6], (D, RANK), D ** -0.5, 0.0625, ((0, 8),)),
        "proj_down_in": noise(arg_keys[7], (FF, RANK), FF ** -0.5, 0.03125, ((0, 8),)),
        "proj_gate_out": noise(arg_keys[8], (FF, RANK), FF ** -0.5, 0.03125, ((0, 8),)),
        "proj_up_out": noise(arg_keys[9], (FF, RANK), FF ** -0.5, 0.03125, ((0, 8),)),
        "proj_down_out": noise(arg_keys[10], (D, RANK), D ** -0.5, 0.0625, ((0, 8),)),
        "example_ids": jax.vmap(lambda own: jnp.searchsorted(jnp.cumsum(ragged_sizes(own, EX_DEV, TOK, 2 * TOK // EX_DEV, 2)), jnp.arange(TOK), side="right"))(jax.random.split(arg_keys[11], GROUPS)).reshape((GROUPS, TOK)).astype(jnp.int32),
        "query_sketches": noise(arg_keys[12], (QUERIES, SKETCH), 0.003, 0.019897461, ((0, 32), (1, 8))),
    }


def project(left, right):
    return jnp.dot(left, right, preferred_element_type=jnp.float32)


def reference(layer_input, hidden_act, grad_gate, grad_up, grad_output, proj_gate_in, proj_up_in, proj_down_in, proj_gate_out, proj_up_out, proj_down_out, example_ids, query_sketches):
    projected = jnp.concatenate([
        project(grad_gate, proj_gate_out), project(grad_up, proj_up_out), project(grad_output, proj_down_out),
        project(layer_input, proj_gate_in), project(layer_input, proj_up_in), project(hidden_act, proj_down_in)], axis=1).astype(jnp.bfloat16)
    blocks = projected.astype(jnp.float32).reshape(GROUPS, TOK, 6 * RANK)

    def one_group(inputs):
        group_block, segment_ids = inputs
        onehot = (segment_ids[:, None] == jnp.arange(EX_DEV, dtype=jnp.int32)[None, :]).astype(jnp.float32)
        pieces = []
        for layer in range(3):
            y_side = group_block[:, layer * RANK:(layer + 1) * RANK]
            x_side = group_block[:, (3 + layer) * RANK:(4 + layer) * RANK]
            outer = (y_side[:, :, None] * x_side[:, None, :]).reshape(TOK, RANK * RANK)
            pieces.append(jnp.dot(onehot.T, outer, precision=lax.Precision.HIGHEST))
        return jnp.concatenate(pieces, axis=1)

    sketches = lax.map(one_group, (blocks, example_ids)).reshape(EXAMPLES, SKETCH).astype(jnp.bfloat16)
    scores = lax.dot_general(sketches, query_sketches, (((1,), (1,)), ((), ())), preferred_element_type=jnp.float32)
    return sketches, scores
```

```python
import jax
import jax.numpy as jnp
from jax import lax
from jax.sharding import Mesh, PartitionSpec as P

EX_DEV = 16
RANK = 64
TENSOR = 8
ROWS = 3 * RANK // TENSOR
DP = ("y", "zhh", "zhl", "core")
S_AXES = ("zhl", "core")
G_AXES = ("y", "zhh")


def project_t(weight, act):
    dims = (((0,), (1,)), ((), ()))
    return lax.dot_general(weight, act, dims, preferred_element_type=jnp.float32)


def gather_sketch(sketch):
    out = sketch[None]
    for axis in reversed(S_AXES):
        other = lax.ppermute(out, axis, [(0, 1), (1, 0)])
        first = lax.axis_index(axis) == 0
        out = jnp.concatenate([jnp.where(first, out, other), jnp.where(first, other, out)], axis=0)
    return out


def per_device(
    layer_input,
    hidden_act,
    grad_gate,
    grad_up,
    grad_output,
    proj_gate_in,
    proj_up_in,
    proj_down_in,
    proj_gate_out,
    proj_up_out,
    proj_down_out,
    example_ids,
    query_sketches,
):
    tok = layer_input.shape[0]
    queries = lax.all_gather(query_sketches, G_AXES, axis=0, tiled=True)
    y_t = jnp.concatenate(
        [
            project_t(proj_gate_out, grad_gate),
            project_t(proj_up_out, grad_up),
            project_t(proj_down_out, grad_output),
        ],
        axis=0,
    ).astype(jnp.bfloat16)
    x_gu = project_t(jnp.concatenate([proj_gate_in, proj_up_in], axis=1), layer_input).astype(jnp.bfloat16)
    x_t = [x_gu[:RANK], x_gu[RANK:], project_t(proj_down_in, hidden_act).astype(jnp.bfloat16)]
    send = []
    for t in range(TENSOR):
        send.append(y_t[ROWS * t : ROWS * (t + 1)])
        send.append(x_t[ROWS * t // RANK])
        send.append(x_t[(ROWS * t + ROWS - 1) // RANK])
    send = jnp.concatenate(send, axis=0)
    got = lax.all_to_all(send, "tensor", 0, 0, tiled=True)
    width = ROWS + 2 * RANK
    summed = jnp.sum(got.reshape(TENSOR, width, tok).astype(jnp.float32), axis=0).astype(jnp.bfloat16)
    one_hot = example_ids == jnp.arange(EX_DEV, dtype=jnp.int32)[:, None]
    masked = jnp.where(one_hot[:, None, :], summed[None, :ROWS], jnp.bfloat16(0)).reshape(EX_DEV * ROWS, tok)
    both = lax.dot_general(
        masked, summed[ROWS:], (((1,), (1,)), ((), ())), preferred_element_type=jnp.float32
    ).reshape(EX_DEV, ROWS, 2 * RANK)
    first_row = lax.axis_index("tensor") * ROWS
    row = first_row + jnp.arange(ROWS, dtype=jnp.int32)
    in_first = (row // RANK == first_row // RANK)[None, :, None]
    sketch = jnp.where(in_first, both[:, :, :RANK], both[:, :, RANK:]).astype(jnp.bfloat16)
    sketch = sketch.reshape(EX_DEV, ROWS * RANK)

    group = gather_sketch(sketch)
    s = group.shape[0]
    partial = lax.dot_general(
        group.reshape(s * EX_DEV, ROWS * RANK),
        queries,
        (((1,), (1,)), ((), ())),
        preferred_element_type=jnp.float32,
    )
    nq = partial.shape[1] // TENSOR
    partial = partial.reshape(s, EX_DEV, TENSOR, nq).transpose(0, 2, 1, 3).reshape(s * TENSOR * EX_DEV, nq)
    back = lax.all_to_all(partial, S_AXES + ("tensor",), 0, 0, tiled=True)
    back = jnp.sum(back.reshape(s, TENSOR, EX_DEV, nq), axis=1)
    if S_AXES == ("zhl", "core"):
        scores = back.transpose(1, 0, 2)
    elif S_AXES == ("core",):
        scores = back.reshape(2, EX_DEV, 2, 128).transpose(1, 2, 0, 3)
    else:
        scores = back.transpose(1, 0, 2)
    return (sketch, scores.reshape(EX_DEV, s * nq))


def solution(mesh):
    split = Mesh(mesh.devices.reshape(4, 2, 2, 2, TENSOR), DP + ("tensor",))
    placed = (P(DP, "tensor"),) * 5 + (P("tensor", None),) * 6 + (P(DP, None), P(DP, "tensor"))
    return jax.shard_map(
        per_device,
        mesh=split,
        in_specs=placed,
        out_specs=(P(DP, "tensor"), P(DP, "tensor")),
        check_vma=False,
    )
```

```python
import functools

import jax
import jax.numpy as jnp
from jax import lax
from jax.experimental import pallas as pl
from jax.experimental.pallas import tpu as pltpu
from jax.sharding import Mesh, PartitionSpec as P

EX_DEV = 16
RANK = 64
TENSOR = 8
ROWS = 24
EXTRA = 8
SLOTS = ROWS + EXTRA
PIECE = SLOTS + RANK
DP = ("y", "zhh", "zhl", "core")
S_AXES = ("zhh", "zhl")
Q_FAR = "relay"
VMEM = 60 << 20

Y_RUNS = (
    ((0, 24), None),
    ((24, 48), None),
    ((48, 64), None, None),
    ((72, 96), (64, 72)),
    ((96, 120), (120, 128)),
    (None, (128, 144), None),
    ((144, 168), None),
    ((168, 192), None),
)
X_OF = (0, 0, 0, 1, 1, 2, 2, 2)


def project_kernel(gg, gu, go, li, ha, wgg, wgu, wgo, wgi, wui, wha, out):
    def dot(a, w):
        return lax.dot_general(a[...], w[...], (((1,), (1,)), ((), ())), preferred_element_type=jnp.float32)

    gate_up = jnp.concatenate([dot(gg, wgg), dot(gu, wgu)], axis=1).T
    down = jnp.concatenate([dot(go, wgo), dot(ha, wha)], axis=1).T
    x_gate_up = jnp.concatenate([dot(li, wgi), dot(li, wui)], axis=1).T.astype(jnp.bfloat16)
    y_t = jnp.concatenate([gate_up, down[:RANK]], axis=0)
    x_t = (x_gate_up[:RANK], x_gate_up[RANK:], down[RANK:].astype(jnp.bfloat16))
    zeros = jnp.zeros((EXTRA, y_t.shape[1]), jnp.float32)
    for t in range(TENSOR):
        runs = [zeros if run is None else y_t[run[0] : run[1]] for run in Y_RUNS[t]]
        out[t, :SLOTS, :] = jnp.concatenate(runs, axis=0).astype(jnp.bfloat16)
        out[t, SLOTS:, :] = x_t[X_OF[t]]


def project(acts, weights):
    tok = acts[0].shape[0]
    step = 128

    def rows(a):
        return pl.BlockSpec((step, a.shape[1]), lambda i: (i, 0))

    def whole(a):
        return pl.BlockSpec(a.shape, lambda i: (0, 0))

    return pl.pallas_call(
        project_kernel,
        grid=(tok // step,),
        in_specs=[rows(a) for a in acts] + [whole(w) for w in weights],
        out_specs=pl.BlockSpec((TENSOR, PIECE, step), lambda i: (0, 0, i)),
        out_shape=jax.ShapeDtypeStruct((TENSOR, PIECE, tok), jnp.bfloat16),
        compiler_params=pltpu.CompilerParams(vmem_limit_bytes=VMEM),
        cost_estimate=pl.CostEstimate(flops=10**9, bytes_accessed=15 << 20, transcendentals=0),
    )(*acts, *weights)


def sketch_kernel(got, ids, out):
    total = got[0].astype(jnp.float32)
    for t in range(1, TENSOR):
        total = total + got[t].astype(jnp.float32)
    tok = total.shape[1]
    x = total[SLOTS:].astype(jnp.bfloat16)
    y = total[:SLOTS].astype(jnp.bfloat16).astype(jnp.float32)
    mask = ids[...] == lax.broadcasted_iota(jnp.int32, (EX_DEV, tok), 0)
    rows = [jnp.where(mask, y[a : a + 1], 0.0).astype(jnp.bfloat16) for a in range(SLOTS)]
    outer = lax.dot_general(
        jnp.concatenate(rows, axis=0), x, (((1,), (1,)), ((), ())), preferred_element_type=jnp.float32
    ).reshape(SLOTS, EX_DEV, RANK)
    for a in range(0, SLOTS, 2):
        pair = jnp.concatenate([outer[a], outer[a + 1]], axis=1)
        out[:, a * RANK : (a + 2) * RANK] = pair.astype(jnp.bfloat16)


def sketch_of(got, ids):
    return pl.pallas_call(
        sketch_kernel,
        out_shape=jax.ShapeDtypeStruct((EX_DEV, SLOTS * RANK), jnp.bfloat16),
        compiler_params=pltpu.CompilerParams(vmem_limit_bytes=32 << 20),
    )(got, ids)


def ring(axis, shift):
    n = lax.axis_size(axis)
    return [(i, (i + shift) % n) for i in range(n)]


def around(x, axis, relay):
    before = lax.ppermute(x, axis, ring(axis, 1))
    after = lax.ppermute(x, axis, ring(axis, -1))
    half = x.shape[1] // 2
    if relay:
        far = (
            lax.ppermute(before[:, :half], axis, ring(axis, 1)),
            lax.ppermute(after[:, half:], axis, ring(axis, -1)),
        )
    else:
        both = lax.ppermute(x, axis, ring(axis, 2))
        far = (both[:, :half], both[:, half:])
    return x, after, far, before


def score_kernel(s0, s1, s2a, s2b, s3, *refs):
    pieces, out = refs[:-1], refs[-1]
    y, core = lax.axis_index("y"), lax.axis_index("core")
    zhh = lax.axis_index("zhh")
    zh = zhh * 2 + lax.axis_index("zhl")
    far = jnp.concatenate([s2a[...], s2b[...]], axis=1)
    group = jnp.concatenate([s0[...], s1[...], far, s3[...]], axis=0)
    out[...] = jnp.zeros(out.shape, out.dtype)
    half = group.shape[1] // 2
    dims = (((1,), (1,)), ((), ()))

    def dot(left, right):
        return lax.dot_general(left, right, dims, preferred_element_type=jnp.float32)

    for c in range(2):
        q0, q1, q2a, q2b, q3 = pieces[5 * c : 5 * c + 5]
        lane = pl.multiple_of(lax.rem(core + c, 2) * 128, 128)
        for r, q in enumerate((q0, q1, (q2a, q2b), q3)):
            if r == 2:
                part = dot(group[:, :half], q2a[...]) + dot(group[:, half:], q2b[...])
            else:
                part = dot(group, q[...])
            part = part.astype(jnp.bfloat16)
            slot = lax.rem(y + r, 4) * 2 + zhh
            for z in range(4):
                out[lax.rem(zh + z, 4), slot, :, pl.ds(lane, 128)] = part[z * EX_DEV : (z + 1) * EX_DEV]


def finish_kernel(back, out):
    zlo = lax.rem(lax.axis_index("tensor"), 2)
    for zhl in range(2):
        total = back[zlo * 2 + zhl, 0].astype(jnp.float32)
        for t in range(1, TENSOR):
            total = total + back[zlo * 2 + zhl, t].astype(jnp.float32)
        out[:, zhl * 256 : (zhl + 1) * 256] = total


def flat(group):
    own, after, far, before = group
    return (own, after) + tuple(far) + (before,)


def per_device(
    layer_input,
    hidden_act,
    grad_gate,
    grad_up,
    grad_output,
    proj_gate_in,
    proj_up_in,
    proj_down_in,
    proj_gate_out,
    proj_up_out,
    proj_down_out,
    example_ids,
    query_sketches,
):
    t = lax.axis_index("tensor")
    acts = (grad_gate, grad_up, grad_output, layer_input, hidden_act)
    weights = (proj_gate_out, proj_up_out, proj_down_out, proj_gate_in, proj_up_in, proj_down_in)
    queries = flat(around(query_sketches, "y", Q_FAR == "relay"))
    others = tuple(lax.ppermute(q, "core", ring("core", 1)) for q in queries)
    send = project(acts, tuple(w.T for w in weights))
    got = lax.all_to_all(send, "tensor", 0, 0, tiled=True)
    wide = sketch_of(got, example_ids)
    main, extra = wide[:, : ROWS * RANK], wide[:, ROWS * RANK :]
    moved = lax.ppermute(extra, "tensor", [(3, 2), (4, 5)])
    none = jnp.zeros_like(moved)
    place = jnp.concatenate([jnp.where(t == 5, moved, none), none, jnp.where(t == 2, moved, none)], axis=1)
    sketch = main + place

    group = flat(around(sketch, S_AXES, False))
    partial = pl.pallas_call(
        score_kernel,
        out_shape=jax.ShapeDtypeStruct((4, TENSOR, EX_DEV, 256), jnp.bfloat16),
        compiler_params=pltpu.CompilerParams(vmem_limit_bytes=32 << 20),
    )(*group, *queries, *others)
    back = lax.all_to_all(partial.reshape(4 * TENSOR, EX_DEV, 256), S_AXES + ("tensor",), 0, 0, tiled=True)
    scores = pl.pallas_call(
        finish_kernel,
        out_shape=jax.ShapeDtypeStruct((EX_DEV, 512), jnp.float32),
        compiler_params=pltpu.CompilerParams(vmem_limit_bytes=32 << 20),
    )(back.reshape(4, TENSOR, EX_DEV, 256))
    return (sketch, scores)


def solution(mesh):
    split = Mesh(mesh.devices.reshape(4, 2, 2, 2, TENSOR), DP + ("tensor",))
    placed = (P(DP, "tensor"),) * 5 + (P("tensor", None),) * 6 + (P(DP, None), P(DP, "tensor"))
    return jax.shard_map(
        per_device,
        mesh=split,
        in_specs=placed,
        out_specs=(P(DP, "tensor"), P(DP, "tensor")),
        check_vma=False,
    )
```

```python
import functools

import jax
import jax.numpy as jnp
from jax import lax
from jax.experimental import pallas as pl
from jax.experimental.pallas import tpu as pltpu
from jax.sharding import Mesh, PartitionSpec as P

EX_DEV = 16
RANK = 64
TENSOR = 8
ROWS = 24
EXTRA = 8
SLOTS = ROWS + EXTRA
PIECE = SLOTS + RANK
DP = ("y", "zhh", "zhl", "core")
S_AXES = ("zhh", "zhl")
VMEM = 60 << 20

Y_RUNS = (
    ((0, 24), None),
    ((24, 48), None),
    ((48, 64), None, None),
    ((72, 96), (64, 72)),
    ((96, 120), (120, 128)),
    (None, (128, 144), None),
    ((144, 168), None),
    ((168, 192), None),
)
X_OF = (0, 0, 0, 1, 1, 2, 2, 2)


def project_kernel(*refs):
    count = len(refs) // 2 - 1
    ins, out, held, sems = refs[:count], refs[count], refs[count + 1 : -1], refs[-1]
    copies = [pltpu.make_async_copy(ins[i], held[i], sems.at[i]) for i in range(count)]
    for copy in copies:
        copy.start()

    def dot(first, last):
        for copy in copies[first:last]:
            copy.wait()
        weight = [held[i][...] for i in range(first, last - 1)]
        weight = weight[0] if len(weight) == 1 else jnp.concatenate(weight, axis=0)
        return lax.dot_general(
            weight, held[last - 1][...], (((1,), (1,)), ((), ())), preferred_element_type=jnp.float32
        )

    gate, up = dot(0, 2), dot(2, 4)
    x_down = dot(4, 6).astype(jnp.bfloat16)
    y_t = jnp.concatenate([gate, up, dot(6, 8)], axis=0)
    x_gate_up = dot(8, 11).astype(jnp.bfloat16)
    x_t = (x_gate_up[:RANK], x_gate_up[RANK:], x_down)
    zeros = jnp.zeros((EXTRA, y_t.shape[1]), jnp.float32)
    for t in range(TENSOR):
        runs = [zeros if run is None else y_t[run[0] : run[1]] for run in Y_RUNS[t]]
        out[t, :SLOTS, :] = jnp.concatenate(runs, axis=0).astype(jnp.bfloat16)
        out[t, SLOTS:, :] = x_t[X_OF[t]]


def project(*operands):
    tok = operands[1].shape[0]
    return pl.pallas_call(
        project_kernel,
        in_specs=[pl.BlockSpec(memory_space=pl.ANY)] * len(operands),
        out_specs=pl.BlockSpec(memory_space=pltpu.VMEM),
        out_shape=jax.ShapeDtypeStruct((TENSOR, PIECE, tok), jnp.bfloat16),
        scratch_shapes=[pltpu.VMEM(a.shape, a.dtype) for a in operands]
        + [pltpu.SemaphoreType.DMA((len(operands),))],
        compiler_params=pltpu.CompilerParams(vmem_limit_bytes=VMEM),
        cost_estimate=pl.CostEstimate(flops=10**9, bytes_accessed=15 << 20, transcendentals=0),
    )(*operands)


def sketch_kernel(got, ids, out):
    total = got[0].astype(jnp.float32)
    for t in range(1, TENSOR):
        total = total + got[t].astype(jnp.float32)
    tok = total.shape[1]
    x = total[SLOTS:].astype(jnp.bfloat16)
    y = total[:SLOTS].astype(jnp.bfloat16).astype(jnp.float32)
    mask = ids[...] == lax.broadcasted_iota(jnp.int32, (EX_DEV, tok), 0)
    rows = [jnp.where(mask, y[a : a + 1], 0.0).astype(jnp.bfloat16) for a in range(SLOTS)]
    outer = lax.dot_general(
        jnp.concatenate(rows, axis=0), x, (((1,), (1,)), ((), ())), preferred_element_type=jnp.float32
    ).reshape(SLOTS, EX_DEV, RANK)
    for a in range(0, SLOTS, 2):
        pair = jnp.concatenate([outer[a], outer[a + 1]], axis=1)
        out[:, a * RANK : (a + 2) * RANK] = pair.astype(jnp.bfloat16)


def sketch_of(got, ids):
    return pl.pallas_call(
        sketch_kernel,
        out_shape=jax.ShapeDtypeStruct((EX_DEV, SLOTS * RANK), jnp.bfloat16),
        compiler_params=pltpu.CompilerParams(vmem_limit_bytes=32 << 20),
    )(got, ids)


def ring(axis, shift):
    n = lax.axis_size(axis)
    return [(i, (i + shift) % n) for i in range(n)]


def around(x, axis, relay):
    before = lax.ppermute(x, axis, ring(axis, 1))
    after = lax.ppermute(x, axis, ring(axis, -1))
    half = x.shape[1] // 2
    if relay:
        far = (
            lax.ppermute(before[:, :half], axis, ring(axis, 1)),
            lax.ppermute(after[:, half:], axis, ring(axis, -1)),
        )
    else:
        both = lax.ppermute(x, axis, ring(axis, 2))
        far = (both[:, :half], both[:, half:])
    return x, after, far, before


def score_kernel(sketches, queries, out):
    y, core = lax.axis_index("y"), lax.axis_index("core")
    zhh = lax.axis_index("zhh")
    group = sketches[...].reshape(4 * EX_DEV, ROWS * RANK)
    out[...] = jnp.zeros(out.shape, out.dtype)
    for c in range(2):
        lane = pl.multiple_of(lax.rem(core + c, 2) * 128, 128)
        for r in range(4):
            part = lax.dot_general(
                group, queries[4 * c + r], (((1,), (1,)), ((), ())), preferred_element_type=jnp.float32
            ).astype(jnp.bfloat16)
            slot = lax.rem(y + r, 4) * 2 + zhh
            for z in range(4):
                out[z, slot, :, pl.ds(lane, 128)] = part[z * EX_DEV : (z + 1) * EX_DEV]


def finish_kernel(back, out):
    zlo = lax.rem(lax.axis_index("tensor"), 2)
    for zhl in range(2):
        total = back[zlo * 2 + zhl, 0].astype(jnp.float32)
        for t in range(1, TENSOR):
            total = total + back[zlo * 2 + zhl, t].astype(jnp.float32)
        out[:, zhl * 256 : (zhl + 1) * 256] = total


def flat(group):
    own, after, far, before = group
    return (own, after) + tuple(far) + (before,)


def per_device(
    layer_input,
    hidden_act,
    grad_gate,
    grad_up,
    grad_output,
    proj_gate_in,
    proj_up_in,
    proj_down_in,
    proj_gate_out,
    proj_up_out,
    proj_down_out,
    example_ids,
    query_sketches,
):
    t = lax.axis_index("tensor")
    before, after = (lax.ppermute(query_sketches, "y", ring("y", shift)) for shift in (1, -1))
    send = project(
        proj_gate_out.T, grad_gate, proj_up_out.T, grad_up, proj_down_in.T, hidden_act,
        proj_down_out.T, grad_output, proj_gate_in.T, proj_up_in.T, layer_input,
    )
    send, before, after = lax.optimization_barrier((send, before, after))
    half = query_sketches.shape[1] // 2
    far = (
        lax.ppermute(before[:, :half], "y", ring("y", 1)),
        lax.ppermute(after[:, half:], "y", ring("y", -1)),
    )
    queries = flat((query_sketches, after, far, before))
    others = tuple(lax.ppermute(q, "core", ring("core", 1)) for q in queries)
    got = lax.all_to_all(send, "tensor", 0, 0, tiled=True)
    got, queries, others = lax.optimization_barrier((got, queries, others))
    wide = sketch_of(got, example_ids)
    main, extra = wide[:, : ROWS * RANK], wide[:, ROWS * RANK :]
    moved = lax.ppermute(extra, "tensor", [(3, 2), (4, 5)])
    none = jnp.zeros_like(moved)
    place = jnp.concatenate([jnp.where(t == 5, moved, none), none, jnp.where(t == 2, moved, none)], axis=1)
    sketch = main + place

    sent, queries, others = lax.optimization_barrier((sketch, queries, others))
    group = lax.all_to_all(jnp.broadcast_to(sent, (4,) + sketch.shape), S_AXES, 0, 0, tiled=True)
    held = []
    for own, after, low, high, before in (queries, others):
        held += [own, after, jnp.concatenate([low, high], axis=1), before]
    held = jnp.stack(held)
    partial = pl.pallas_call(
        score_kernel,
        out_shape=jax.ShapeDtypeStruct((4, TENSOR, EX_DEV, 256), jnp.bfloat16),
        compiler_params=pltpu.CompilerParams(vmem_limit_bytes=32 << 20),
    )(group, held)
    back = lax.all_to_all(partial.reshape(4 * TENSOR, EX_DEV, 256), S_AXES + ("tensor",), 0, 0, tiled=True)
    scores = pl.pallas_call(
        finish_kernel,
        out_shape=jax.ShapeDtypeStruct((EX_DEV, 512), jnp.float32),
        compiler_params=pltpu.CompilerParams(vmem_limit_bytes=32 << 20),
    )(back.reshape(4, TENSOR, EX_DEV, 256))
    return (sketch, scores)


def solution(mesh):
    split = Mesh(mesh.devices.reshape(4, 2, 2, 2, TENSOR), DP + ("tensor",))
    placed = (P(DP, "tensor"),) * 5 + (P("tensor", None),) * 6 + (P(DP, None), P(DP, "tensor"))
    return jax.shard_map(
        per_device,
        mesh=split,
        in_specs=placed,
        out_specs=(P(DP, "tensor"), P(DP, "tensor")),
        check_vma=False,
    )
```

```python
import functools

import jax
import jax.numpy as jnp
from jax import lax
from jax.experimental import pallas as pl
from jax.experimental.pallas import tpu as pltpu
from jax.sharding import Mesh, PartitionSpec as P

EX_DEV = 16
RANK = 64
TENSOR = 8
ROWS = 24
EXTRA = 8
SLOTS = ROWS + EXTRA
PIECE = SLOTS + RANK
DP = ("y", "zhh", "zhl", "core")
S_AXES = ("zhh", "zhl")
VMEM = 60 << 20

Y_RUNS = (
    ((0, 24), None),
    ((24, 48), None),
    ((48, 64), None, None),
    ((72, 96), (64, 72)),
    ((96, 120), (120, 128)),
    (None, (128, 144), None),
    ((144, 168), None),
    ((168, 192), None),
)
X_OF = (0, 0, 0, 1, 1, 2, 2, 2)


def project_kernel(*refs):
    count = len(refs) // 2 - 1
    ins, out, held, sems = refs[:count], refs[count], refs[count + 1 : -1], refs[-1]
    copies = [pltpu.make_async_copy(ins[i], held[i], sems.at[i]) for i in range(count)]
    for copy in copies:
        copy.start()

    def dot(first, last):
        for copy in copies[first:last]:
            copy.wait()
        weight = [held[i][...] for i in range(first, last - 1)]
        weight = weight[0] if len(weight) == 1 else jnp.concatenate(weight, axis=0)
        return lax.dot_general(
            weight, held[last - 1][...], (((1,), (1,)), ((), ())), preferred_element_type=jnp.float32
        )

    gate, up = dot(0, 2), dot(2, 4)
    x_down = dot(4, 6).astype(jnp.bfloat16)
    y_t = jnp.concatenate([gate, up, dot(6, 8)], axis=0)
    x_gate_up = dot(8, 11).astype(jnp.bfloat16)
    x_t = (x_gate_up[:RANK], x_gate_up[RANK:], x_down)
    zeros = jnp.zeros((EXTRA, y_t.shape[1]), jnp.float32)
    for t in range(TENSOR):
        runs = [zeros if run is None else y_t[run[0] : run[1]] for run in Y_RUNS[t]]
        out[t, :SLOTS, :] = jnp.concatenate(runs, axis=0).astype(jnp.bfloat16)
        out[t, SLOTS:, :] = x_t[X_OF[t]]


def project(*operands):
    tok = operands[1].shape[0]
    return pl.pallas_call(
        project_kernel,
        in_specs=[pl.BlockSpec(memory_space=pl.ANY)] * len(operands),
        out_specs=pl.BlockSpec(memory_space=pltpu.VMEM),
        out_shape=jax.ShapeDtypeStruct((TENSOR, PIECE, tok), jnp.bfloat16),
        scratch_shapes=[pltpu.VMEM(a.shape, a.dtype) for a in operands]
        + [pltpu.SemaphoreType.DMA((len(operands),))],
        compiler_params=pltpu.CompilerParams(vmem_limit_bytes=VMEM),
        cost_estimate=pl.CostEstimate(flops=10**9, bytes_accessed=15 << 20, transcendentals=0),
    )(*operands)


def sketch_kernel(got, ids, out):
    total = got[0].astype(jnp.float32)
    for t in range(1, TENSOR):
        total = total + got[t].astype(jnp.float32)
    tok = total.shape[1]
    x = total[SLOTS:].astype(jnp.bfloat16)
    y = total[:SLOTS].astype(jnp.bfloat16).astype(jnp.float32)
    mask = ids[...] == lax.broadcasted_iota(jnp.int32, (EX_DEV, tok), 0)
    rows = [jnp.where(mask, y[a : a + 1], 0.0).astype(jnp.bfloat16) for a in range(SLOTS)]
    outer = lax.dot_general(
        jnp.concatenate(rows, axis=0), x, (((1,), (1,)), ((), ())), preferred_element_type=jnp.float32
    ).reshape(SLOTS, EX_DEV, RANK)
    for a in range(0, SLOTS, 2):
        pair = jnp.concatenate([outer[a], outer[a + 1]], axis=1)
        out[:, a * RANK : (a + 2) * RANK] = pair.astype(jnp.bfloat16)


def sketch_of(got, ids):
    return pl.pallas_call(
        sketch_kernel,
        out_shape=jax.ShapeDtypeStruct((EX_DEV, SLOTS * RANK), jnp.bfloat16),
        compiler_params=pltpu.CompilerParams(vmem_limit_bytes=32 << 20),
    )(got, ids)


def ring(axis, shift):
    n = lax.axis_size(axis)
    return [(i, (i + shift) % n) for i in range(n)]


def around(x, axis, relay):
    before = lax.ppermute(x, axis, ring(axis, 1))
    after = lax.ppermute(x, axis, ring(axis, -1))
    half = x.shape[1] // 2
    if relay:
        far = (
            lax.ppermute(before[:, :half], axis, ring(axis, 1)),
            lax.ppermute(after[:, half:], axis, ring(axis, -1)),
        )
    else:
        both = lax.ppermute(x, axis, ring(axis, 2))
        far = (both[:, :half], both[:, half:])
    return x, after, far, before


def score_kernel(sketches, queries, out):
    y, core = lax.axis_index("y"), lax.axis_index("core")
    zhh = lax.axis_index("zhh")
    group = sketches[...].reshape(4 * EX_DEV, ROWS * RANK)
    out[...] = jnp.zeros(out.shape, out.dtype)
    for c in range(2):
        lane = pl.multiple_of(lax.rem(core + c, 2) * 128, 128)
        for r in range(4):
            part = lax.dot_general(
                group, queries[4 * c + r], (((1,), (1,)), ((), ())), preferred_element_type=jnp.float32
            ).astype(jnp.bfloat16)
            slot = lax.rem(y + r, 4) * 2 + zhh
            for z in range(4):
                out[z, slot, :, pl.ds(lane, 128)] = part[z * EX_DEV : (z + 1) * EX_DEV]


def finish_kernel(back, out):
    zlo = lax.rem(lax.axis_index("tensor"), 2)
    for zhl in range(2):
        total = back[zlo * 2 + zhl, 0].astype(jnp.float32)
        for t in range(1, TENSOR):
            total = total + back[zlo * 2 + zhl, t].astype(jnp.float32)
        out[:, zhl * 256 : (zhl + 1) * 256] = total


def flat(group):
    own, after, far, before = group
    return (own, after) + tuple(far) + (before,)


def per_device(
    layer_input,
    hidden_act,
    grad_gate,
    grad_up,
    grad_output,
    proj_gate_in,
    proj_up_in,
    proj_down_in,
    proj_gate_out,
    proj_up_out,
    proj_down_out,
    example_ids,
    query_sketches,
):
    t = lax.axis_index("tensor")
    before, after = (lax.ppermute(query_sketches, "y", ring("y", shift)) for shift in (1, -1))
    send = project(
        proj_gate_out.T, grad_gate, proj_up_out.T, grad_up, proj_down_in.T, hidden_act,
        proj_down_out.T, grad_output, proj_gate_in.T, proj_up_in.T, layer_input,
    )
    send, before, after = lax.optimization_barrier((send, before, after))
    half = query_sketches.shape[1] // 2
    far = (
        lax.ppermute(before[:, :half], "y", ring("y", 1)),
        lax.ppermute(after[:, half:], "y", ring("y", -1)),
    )
    queries = flat((query_sketches, after, far, before))
    others = tuple(lax.ppermute(q, "core", ring("core", 1)) for q in queries)
    got = lax.all_to_all(send, "tensor", 0, 0, tiled=True)
    got, _ = lax.optimization_barrier((got, far))
    wide = sketch_of(got, example_ids)
    main, extra = wide[:, : ROWS * RANK], wide[:, ROWS * RANK :]
    moved = lax.ppermute(extra, "tensor", [(3, 2), (4, 5)])
    none = jnp.zeros_like(moved)
    place = jnp.concatenate([jnp.where(t == 5, moved, none), none, jnp.where(t == 2, moved, none)], axis=1)
    sketch = main + place

    sent, queries, others = lax.optimization_barrier((sketch, queries, others))
    group = lax.all_to_all(jnp.broadcast_to(sent, (4,) + sketch.shape), S_AXES, 0, 0, tiled=True)
    held = []
    for own, after, low, high, before in (queries, others):
        held += [own, after, jnp.concatenate([low, high], axis=1), before]
    held = jnp.stack(held)
    partial = pl.pallas_call(
        score_kernel,
        out_shape=jax.ShapeDtypeStruct((4, TENSOR, EX_DEV, 256), jnp.bfloat16),
        compiler_params=pltpu.CompilerParams(vmem_limit_bytes=32 << 20),
    )(group, held)
    back = lax.all_to_all(partial.reshape(4 * TENSOR, EX_DEV, 256), S_AXES + ("tensor",), 0, 0, tiled=True)
    scores = pl.pallas_call(
        finish_kernel,
        out_shape=jax.ShapeDtypeStruct((EX_DEV, 512), jnp.float32),
        compiler_params=pltpu.CompilerParams(vmem_limit_bytes=32 << 20),
    )(back.reshape(4, TENSOR, EX_DEV, 256))
    return (sketch, scores)


def solution(mesh):
    split = Mesh(mesh.devices.reshape(4, 2, 2, 2, TENSOR), DP + ("tensor",))
    placed = (P(DP, "tensor"),) * 5 + (P("tensor", None),) * 6 + (P(DP, None), P(DP, "tensor"))
    return jax.shard_map(
        per_device,
        mesh=split,
        in_specs=placed,
        out_specs=(P(DP, "tensor"), P(DP, "tensor")),
        check_vma=False,
    )
```
